512 devices in a mesh: dp: 4 (over z_lo, core), ctx: 32 (over y, z_hi), tp: 4 (over x).
Axes of the slice: x: 4, y: 8, z: 8 (z_hi: 4, z_lo: 2; z = z_hi * 2 + z_lo), core: 2. Of those that a mesh axis runs over, the one named last changes fastest.
Arguments:
- queries_raw: bfloat16 [4, 8192, 4096], P('dp', 'ctx', 'tp'), may hold values from -400 to 400
- keys_raw: bfloat16 [4, 8192, 512], P('dp', 'ctx', 'tp'), may hold values from -400 to 400
- values: bfloat16 [4, 8192, 512], P('dp', 'ctx', 'tp'), may hold values from -6 to 6
- grad_out: bfloat16 [4, 8192, 4096], P('dp', 'ctx', 'tp'), may hold values from -6 to 6
- q_gain: float32 [128], replicated, may hold values from 0.5 to 8
- k_gain: float32 [128], replicated, may hold values from 0.5 to 8
- doc_lengths: int32 [4, 64], P('dp'), may hold values from 1 to 1024, 8192 in all within a row
Outputs:
- queries_grad: bfloat16 [4, 8192, 4096], P('dp', 'ctx', 'tp')
- keys_grad: bfloat16 [4, 8192, 512], P('dp', 'ctx', 'tp')
- values_grad: bfloat16 [4, 8192, 512], P('dp', 'ctx', 'tp')
- gain_grads: float32 [2, 128], replicated
The draws below stay inside these ranges and needn't reach their ends.
Inputs may be any that keep to these rules, and one draw needn't show every extreme that they name: `doc_lengths`: each pack's documents lie end to end and fill its 8192 tokens.
All inputs are finite; a program needn't handle non-finite values.
Results may differ from the reference program's by a relative error of at most 0.024.
The reference program's roundings to bfloat16 on the way (of `q_rot`, `k_rot`, `weights_b` and `score_grad`) count: a program that leaves them out, or rounds other values in their place, can miss the bound.
Values may be sent and summed in bfloat16 or wider, within the bound.
No kernel may reach another device: no remote copies, remote signals or barrier semaphores. Data moves between devices by JAX's collectives and lax.ppermute only.
A program may use at most 64 MiB of HBM per device.

```python
import math
import jax
import jax.numpy as jnp
import numpy as np
from jax import lax

HD = 128
QH = 32
KVH = 4
TOK_DEV = 256
REACH = 4
PACKS = 4
SEQ = 8192
MAXDOC = 1024
DOCS = 64
N_CTX = 32


def scaled_normal(key, heads):
    key_base, key_row, key_col = jax.random.split(key, 3)
    base_draw = jax.random.truncated_normal(key_base, -4.0, 4.0, (PACKS, SEQ, heads, HD), jnp.float32)
    row_scale = jnp.exp(jax.random.uniform(key_row, (PACKS, SEQ, heads, 1), jnp.float32) * math.log(10.0))
    col_scale = jnp.exp(jax.random.uniform(key_col, (1, 1, heads, HD), jnp.float32) * math.log(10.0))
    return base_draw * row_scale * col_scale


def draw_queries_raw(key, part):
    key = jax.random.fold_in(key, 11)
    draw_key = jax.random.fold_in(key, 0)
    result = scaled_normal(draw_key, QH)
    return result.reshape(PACKS, SEQ, QH * HD).astype(jnp.bfloat16)


def draw_keys_raw(key, part):
    key = jax.random.fold_in(key, 23)
    draw_key = jax.random.fold_in(key, 0)
    result = scaled_normal(draw_key, KVH)
    return result.reshape(PACKS, SEQ, KVH * HD).astype(jnp.bfloat16)


def draw_q_gain(key, part):
    key = jax.random.fold_in(key, 31)
    return jax.random.uniform(key, (HD,), jnp.float32, 0.5, 1.5)


def draw_k_gain(key, part):
    key = jax.random.fold_in(key, 41)
    return jax.random.uniform(key, (HD,), jnp.float32, 0.5, 1.5)


def steps_of(key, dims, shards, least, largest):
    def one(dim, parts):
        steps = jax.random.uniform(jax.random.fold_in(jax.random.fold_in(key, 6), dim), (parts,), jnp.float32, least / len(shards), largest / len(shards))
        return jnp.repeat(jnp.exp(steps), dims[dim] // parts).reshape((-1,) + (1,) * (len(dims) - dim - 1))

    gain = one(*shards[0])
    for cut in shards[1:]:
        gain = gain * one(*cut)
    return gain


def profile(number_of, total, reach, slope):
    loads = [(1 << 20) // math.isqrt(grade ** slope) + 1 for grade in range(2, number_of + 1)]
    rest, holding = total - reach - (number_of - 1), [1] * (number_of - 1)
    while rest > 0:
        free = [i for i in range(number_of - 1) if holding[i] < reach]
        whole, budget = sum([loads[i] for i in free]), rest
        for i in free:
            addition = min(reach - holding[i], max(1, budget * loads[i] // whole), rest)
            holding[i] = holding[i] + addition
            rest = rest - addition
    return np.array([reach] + holding)


def ragged_sizes(stream_key, count, total, bound, lean):
    if count == 2:
        one = jax.random.randint(stream_key, (), max(1, total - bound), min(bound, total - 1) + 1)
        return jnp.stack([one, total - one])
    sizes = jnp.asarray(profile(count, total, bound, lean), jnp.int32)
    twos = (count - 1) // 2
    source_of, sink = sizes[1:1 + 2 * twos:2], sizes[2:2 + 2 * twos:2]
    slack = jnp.minimum(source_of - 1, bound - sink)
    moved = jax.random.randint(jax.random.fold_in(stream_key, 1), (twos,), 0, 1 << 20) % (slack + 1)
    sizes = sizes.at[1:1 + 2 * twos:2].set(source_of - moved).at[2:2 + 2 * twos:2].set(sink + moved)
    return sizes[jax.random.permutation(jax.random.fold_in(stream_key, 2), count)]


def normal_values(stream_key, shape, scale, most, cuts=(), kind=jnp.bfloat16):
    values = jax.random.normal(stream_key, shape, jnp.float32) * scale
    if len(cuts) > 0:
        values = steps_of(stream_key, shape, cuts, -0.22, 0.18) * values
    return jnp.clip(values, min=-most, max=most).astype(kind)


def setup_inputs(seed: int = 0) -> dict:
    splits = jax.random.split(jax.random.key(seed), 8)
    queries_raw = draw_queries_raw(jax.random.fold_in(splits[7], 71), 0)
    keys_raw = draw_keys_raw(jax.random.fold_in(splits[7], 71), 0)
    values = normal_values(splits[2], (PACKS, SEQ, KVH * HD), 1.0, 6.0, ((0, 4), (1, 32), (2, 4)))
    grad_out = normal_values(splits[3], (PACKS, SEQ, QH * HD), 1.0, 6.0, ((0, 4), (1, 32), (2, 4)))
    q_gain = draw_q_gain(jax.random.fold_in(splits[7], 71), 0)
    k_gain = draw_k_gain(jax.random.fold_in(splits[7], 71), 0)
    doc_lengths = jax.vmap(lambda own: ragged_sizes(own, DOCS, SEQ, MAXDOC, 2))(jax.random.split(splits[6], PACKS)).reshape((PACKS, DOCS)).astype(jnp.int32)
    return {"queries_raw": queries_raw, "keys_raw": keys_raw, "values": values, "grad_out": grad_out, "q_gain": q_gain, "k_gain": k_gain, "doc_lengths": doc_lengths}


EPSILON = 1e-06
ROPE_BASE = 1000000.0

def locate(tok_index, starts):
    within = starts[None, :] <= tok_index[:, None]
    doc_id = lax.optimization_barrier(jnp.sum(within.astype(jnp.int32), axis=1)).astype(jnp.int32) - 1
    doc_start = lax.optimization_barrier(jnp.max(jnp.where(within, starts[None, :], 0), axis=1)).astype(jnp.int32)
    return (doc_id, (tok_index - doc_start).astype(jnp.int32))

def rotation(position, head_width):
    half_width = head_width // 2
    inv_freq = jnp.exp(jnp.arange(half_width, dtype=jnp.float32) * (-2.0 * math.log(ROPE_BASE) / head_width))
    angles = position.astype(jnp.float32)[:, None] * inv_freq[None, :]
    return (jnp.cos(angles)[:, None, :], jnp.sin(angles)[:, None, :])

def norm_rope(source, gain_vec, cos_part, sine_part):
    values32 = source.astype(jnp.float32)
    inv_rms = lax.rsqrt(lax.optimization_barrier(jnp.mean(values32 * values32, axis=-1, keepdims=True)) + EPSILON)
    normed = values32 * inv_rms
    scaled = normed * gain_vec
    half_width = scaled.shape[-1] // 2
    lower = scaled[..., :half_width]
    upper = scaled[..., half_width:]
    rotated = jnp.concatenate([lower * cos_part - upper * sine_part, upper * cos_part + lower * sine_part], axis=-1)
    return (rotated, normed, inv_rms)

def unrope_norm(rot_grad, gain_vec, normed, inv_rms, cos_part, sine_part):
    half_width = rot_grad.shape[-1] // 2
    grad_lower = rot_grad[..., :half_width]
    grad_upper = rot_grad[..., half_width:]
    norm_grad = jnp.concatenate([grad_lower * cos_part + grad_upper * sine_part, grad_upper * cos_part - grad_lower * sine_part], axis=-1)
    gain_term = lax.optimization_barrier(jnp.sum(norm_grad * normed, axis=(0, 1)))
    gained = norm_grad * gain_vec
    raw_grad = (gained - normed * lax.optimization_barrier(jnp.mean(gained * normed, axis=-1, keepdims=True))) * inv_rms
    return (raw_grad, gain_term)

def attend(q_rot, grad_rows, window_keys, window_values, allowed):
    tok_rows, q_heads, head_width = q_rot.shape
    key_count, kv_heads, _ = window_keys.shape
    group_size = q_heads // kv_heads
    unit_count = q_heads // 2
    score_scale = head_width ** (-0.5)

    def by_units(tensor):
        return tensor.reshape(tok_rows, unit_count, 2, head_width).transpose(1, 2, 0, 3).reshape(unit_count, 2 * tok_rows, head_width)
    unit_keys = jnp.repeat(window_keys.transpose(1, 0, 2), group_size // 2, axis=0)
    unit_values = jnp.repeat(window_values.transpose(1, 0, 2), group_size // 2, axis=0)

    def one_unit(operands):
        queries, gradient, keyset, valueset = operands
        scores = jnp.dot(queries, keyset.T, preferred_element_type=jnp.float32).reshape(2, tok_rows, key_count) * score_scale
        scores = jnp.where(allowed[None], scores, -1e+30)
        row_max = lax.optimization_barrier(jnp.max(scores, axis=-1, keepdims=True))
        row_sum = lax.optimization_barrier(jnp.sum(jnp.exp(scores - row_max), axis=-1, keepdims=True))
        weights = jnp.exp(scores - (row_max + jnp.log(row_sum)))
        weights_b = weights.astype(jnp.bfloat16).reshape(2 * tok_rows, key_count)
        attn_out = jnp.dot(weights_b, valueset, preferred_element_type=jnp.float32)
        row_delta = lax.optimization_barrier(jnp.sum(gradient.astype(jnp.float32) * attn_out, axis=-1)).reshape(2, tok_rows, 1)
        weight_grad = jnp.dot(gradient, valueset.T, preferred_element_type=jnp.float32).reshape(2, tok_rows, key_count)
        score_grad = (weights * (weight_grad - row_delta) * score_scale).astype(jnp.bfloat16).reshape(2 * tok_rows, key_count)
        q_grad = jnp.dot(score_grad, keyset, preferred_element_type=jnp.float32)
        k_grad = jnp.dot(score_grad.T, queries, preferred_element_type=jnp.float32)
        v_grad = jnp.dot(weights_b.T, gradient, preferred_element_type=jnp.float32)
        return (q_grad, k_grad, v_grad)
    q_grad, k_grad, v_grad = lax.map(one_unit, (by_units(q_rot), by_units(grad_rows), unit_keys, unit_values))
    q_grad = q_grad.reshape(unit_count, 2, tok_rows, head_width).transpose(2, 0, 1, 3).reshape(tok_rows, q_heads, head_width)
    k_grad = k_grad.reshape(kv_heads, group_size // 2, key_count, head_width).sum(axis=1).transpose(1, 0, 2)
    v_grad = v_grad.reshape(kv_heads, group_size // 2, key_count, head_width).sum(axis=1).transpose(1, 0, 2)
    return (q_grad, k_grad, v_grad)

def reference(queries_raw, keys_raw, values, grad_out, q_gain, k_gain, doc_lengths):
    reach_back = min(REACH, N_CTX - 1)
    pad_rows = reach_back * TOK_DEV
    window_len = pad_rows + TOK_DEV

    def one_pack(operands):
        q_source, k_source, v_source, g_source, lengths = operands
        seq_len = q_source.shape[0]
        starts = (jnp.cumsum(lengths) - lengths).astype(jnp.int32)
        tok_index = jnp.arange(seq_len, dtype=jnp.int32)
        doc_id, position = locate(tok_index, starts)
        cos_part, sine_part = rotation(position, HD)
        q_rot, q_normed, q_inv = norm_rope(q_source.reshape(seq_len, QH, HD), q_gain, cos_part, sine_part)
        k_rot, k_normed, k_inv = norm_rope(k_source.reshape(seq_len, KVH, HD), k_gain, cos_part, sine_part)
        q_bf = q_rot.astype(jnp.bfloat16)
        k_bf = k_rot.astype(jnp.bfloat16)
        g_rows = g_source.reshape(seq_len, QH, HD)
        k_pad = jnp.concatenate([jnp.zeros((pad_rows, KVH, HD), jnp.bfloat16), k_bf], axis=0)
        v_pad = jnp.concatenate([jnp.zeros((pad_rows, KVH, HD), jnp.bfloat16), v_source.reshape(seq_len, KVH, HD)], axis=0)
        doc_pad = jnp.concatenate([jnp.full((pad_rows,), -1, jnp.int32), doc_id], axis=0)
        local_q = jnp.arange(TOK_DEV, dtype=jnp.int32) + pad_rows
        local_k = jnp.arange(window_len, dtype=jnp.int32)

        def block_step(accums, shard_index):
            k_acc, v_acc = accums
            first_row = (shard_index * TOK_DEV).astype(jnp.int32)
            q_block = lax.dynamic_slice_in_dim(q_bf, first_row, TOK_DEV, 0)
            g_block = lax.dynamic_slice_in_dim(g_rows, first_row, TOK_DEV, 0)
            doc_q = lax.dynamic_slice_in_dim(doc_id, first_row, TOK_DEV, 0)
            keys_here = lax.dynamic_slice_in_dim(k_pad, first_row, window_len, 0)
            vals_here = lax.dynamic_slice_in_dim(v_pad, first_row, window_len, 0)
            doc_k = lax.dynamic_slice_in_dim(doc_pad, first_row, window_len, 0)
            allowed = (doc_k[None, :] == doc_q[:, None]) & (local_k[None, :] <= local_q[:, None])
            q_grad, k_grad, v_grad = attend(q_block, g_block, keys_here, vals_here, allowed)
            k_acc = lax.dynamic_update_slice_in_dim(k_acc, lax.dynamic_slice_in_dim(k_acc, first_row, window_len, 0) + k_grad, first_row, 0)
            v_acc = lax.dynamic_update_slice_in_dim(v_acc, lax.dynamic_slice_in_dim(v_acc, first_row, window_len, 0) + v_grad, first_row, 0)
            return ((k_acc, v_acc), q_grad)
        zero_acc = jnp.zeros((pad_rows + seq_len, KVH, HD), jnp.float32)
        (k_acc, v_acc), q_grads = lax.scan(block_step, (zero_acc, zero_acc), jnp.arange(N_CTX, dtype=jnp.int32))
        q_rot_grad = q_grads.reshape(seq_len, QH, HD)
        q_raw_grad, q_term = unrope_norm(q_rot_grad, q_gain, q_normed, q_inv, cos_part, sine_part)
        k_raw_grad, k_term = unrope_norm(k_acc[pad_rows:], k_gain, k_normed, k_inv, cos_part, sine_part)
        return (q_raw_grad.astype(jnp.bfloat16).reshape(seq_len, QH * HD), k_raw_grad.astype(jnp.bfloat16).reshape(seq_len, KVH * HD), v_acc[pad_rows:].astype(jnp.bfloat16).reshape(seq_len, KVH * HD), jnp.stack([q_term, k_term]))
    results = lax.map(one_pack, (queries_raw, keys_raw, values, grad_out, doc_lengths))
    gain_grads = lax.optimization_barrier(jnp.sum(results[3], axis=0)) * (PACKS * SEQ) ** (-0.5)
    return (results[0], results[1], results[2], gain_grads)
```

```python
import functools
import math

import jax
import jax.numpy as jnp
import numpy as np
from jax import lax
from jax.experimental import pallas as pl
from jax.experimental.pallas import tpu as pltpu
from jax.sharding import Mesh
from jax.sharding import PartitionSpec as P

REACH = 4
EPSILON = 1e-06
ROPE_BASE = 1000000.0
HD = 128
HALF = HD // 2
BLOCKS = REACH + 1
HEADS_PER_STEP = 2
MASKED = -1e30
LOG2E = 1.4426950408889634


def rope_tables(rows):
    freq = ROPE_BASE ** (-2.0 * np.arange(HALF, dtype=np.float64) / HD)
    offsets = np.concatenate([np.arange(rows) - rows * d for d in range(1, REACH + 1)])
    angles = offsets[:, None].astype(np.float64) * np.concatenate([freq, freq])[None, :]
    return np.cos(angles).astype(np.float32), np.sin(angles).astype(np.float32)


def half_sign():
    lane = lax.broadcasted_iota(jnp.int32, (1, HD), 1)
    return jnp.where(lane < HALF, -1.0, 1.0).astype(jnp.float32)


def prep_kernel(rows, docs, lens_ref, first_ref, freq_ref, tabc_ref, tabs_ref, cos_ref, sin_ref, low_ref, scal_ref):
    first = first_ref[0]
    tok_col = lax.broadcasted_iota(jnp.int32, (rows, HD), 0)
    tok_row = lax.broadcasted_iota(jnp.int32, (8, rows), 1)

    def one_doc(d, carry):
        start, reaching, col, row = carry
        rel = start - first
        reaching = jnp.where(rel <= 0, rel, reaching)
        col = jnp.where(tok_col >= rel, rel, col)
        row = jnp.where(tok_row >= rel, rel, row)
        return start + lens_ref[0, d], reaching, col, row

    zero = jnp.int32(0)
    _, reaching, col, row = lax.fori_loop(
        0, docs, one_doc, (zero, zero, jnp.zeros((rows, HD), jnp.int32), jnp.zeros((8, rows), jnp.int32))
    )
    before = -reaching
    scal_ref[0] = before
    scal_ref[1] = 1 + (before + rows - 1) // rows
    low_ref[...] = row
    sign = half_sign()
    freq = freq_ref[...]
    angles = (tok_col - col).astype(jnp.float32) * freq
    cos_ref[0:rows, :] = jnp.cos(angles)
    sin_ref[0:rows, :] = jnp.sin(angles) * sign
    shift = before.astype(jnp.float32) * freq
    shift_c, shift_s = jnp.cos(shift), jnp.sin(shift)
    tab_c, tab_s = tabc_ref[...], tabs_ref[...]
    cos_ref[rows:, :] = shift_c * tab_c - shift_s * tab_s
    sin_ref[rows:, :] = (shift_s * tab_c + shift_c * tab_s) * sign


def normed_of(source):
    values32 = source.astype(jnp.float32)
    inv = lax.rsqrt(jnp.mean(values32 * values32, axis=-1, keepdims=True) + EPSILON)
    return values32 * inv, inv


def rope(scaled, cos, sin):
    return scaled * cos + pltpu.roll(scaled, HALF, 1) * sin


def unrope(grad, cos, sin):
    return grad * cos - pltpu.roll(grad, HALF, 1) * sin


def fold(terms):
    return jnp.sum(terms.reshape(terms.shape[0] // 8, 8, HD), axis=0)


def main_kernel(
    rows, fan,
    scal_ref, low_ref, cos_ref, sin_ref, qgain_ref, kgain_ref, w0, w1, w2, w3, w4, q_ref, g_ref,
    dq_ref, own_ref, o1, o2, o3, o4, gains_ref,
    krot, vwin, knorm, bias, dk, dv, qterm,
):
    step = pl.program_id(0)
    count = scal_ref[1]
    window = (w0, w1, w2, w3, w4)
    heads = q_ref.shape[1] // HD
    scale = HD ** (-0.5)

    @pl.when(step == 0)
    def _():
        qterm[...] = jnp.zeros_like(qterm)
        for d in range(BLOCKS):
            at = slice(d * rows, (d + 1) * rows)

            @pl.when(d < count)
            def _():
                normed, _ = normed_of(window[d][:, :HD])
                knorm[at, :] = normed
                krot[at, :] = rope(normed * kgain_ref[...], cos_ref[at, :], sin_ref[at, :]).astype(jnp.bfloat16)
                vwin[at, :] = window[d][:, HD:]
                dk[at, :] = jnp.zeros((rows, HD), jnp.float32)
                dv[at, :] = jnp.zeros((rows, HD), jnp.float32)
                key = lax.broadcasted_iota(jnp.int32, (rows, rows), 0) - d * rows
                tok = lax.broadcasted_iota(jnp.int32, (rows, rows), 1)
                kept = key >= low_ref[0:1, :]
                if d == 0:
                    kept = kept & (key <= tok)
                bias[at, :] = jnp.where(kept, 0.0, MASKED)

    def attend(blocks):
        size = blocks * rows
        for h in range(heads):
            lanes = slice(h * HD, (h + 1) * HD)
            cos, sin = cos_ref[0:rows, :], sin_ref[0:rows, :]
            q_normed, q_inv = normed_of(q_ref[:, lanes])
            q_rot = rope(q_normed * qgain_ref[...], cos, sin).astype(jnp.bfloat16)
            grad = g_ref[:, lanes]
            keys, vals = krot[0:size, :], vwin[0:size, :]
            across = (((1,), (1,)), ((), ()))
            scores = lax.dot_general(keys, q_rot, across, preferred_element_type=jnp.float32) + bias[0:size, :]
            top = jnp.max(scores, axis=0, keepdims=True)
            power = jnp.exp2((scores - top) * (scale * LOG2E))
            inv_sum = 1.0 / jnp.sum(power, axis=0, keepdims=True)
            wgrad = lax.dot_general(vals, grad, across, preferred_element_type=jnp.float32)
            delta = jnp.sum(power * wgrad, axis=0, keepdims=True) * inv_sum
            weights = power * inv_sum
            sgrad = (weights * (wgrad - delta)).astype(jnp.bfloat16)
            dv[0:size, :] += jnp.dot(weights.astype(jnp.bfloat16), grad, preferred_element_type=jnp.float32)
            dk[0:size, :] += jnp.dot(sgrad, q_rot, preferred_element_type=jnp.float32)
            q_grad = lax.dot_general(sgrad, keys, (((0,), (0,)), ((), ())), preferred_element_type=jnp.float32)
            norm_grad = unrope(q_grad * scale, cos, sin)
            qterm[...] += fold(norm_grad * q_normed)
            gained = norm_grad * qgain_ref[...]
            mean = jnp.mean(gained * q_normed, axis=-1, keepdims=True)
            dq_ref[:, lanes] = ((gained - q_normed * mean) * q_inv).astype(jnp.bfloat16)

    for blocks in range(1, BLOCKS + 1):
        pl.when(count == blocks)(functools.partial(attend, blocks))

    @pl.when(step == pl.num_programs(0) - 1)
    def _():
        kterm = jnp.zeros((8, HD), jnp.float32)
        outs = (own_ref, o1, o2, o3, o4)
        for d in range(BLOCKS):
            at = slice(d * rows, (d + 1) * rows)

            def block_term():
                key_grad = dk[at, :] * scale
                outs[d][:, :HD] = key_grad.astype(outs[d].dtype)
                outs[d][:, HD:] = dv[at, :].astype(outs[d].dtype)
                norm_grad = unrope(key_grad, cos_ref[at, :], sin_ref[at, :])
                return fold(norm_grad * knorm[at, :])

            def no_term():
                outs[d][...] = jnp.zeros_like(outs[d])
                return jnp.zeros((8, HD), jnp.float32)

            kterm = kterm + (block_term() if d == 0 else lax.cond(d < count, block_term, no_term))
        both = jnp.concatenate(
            [jnp.sum(qterm[...], axis=0, keepdims=True), jnp.sum(kterm, axis=0, keepdims=True)], axis=0
        )
        gains_ref[...] = jnp.broadcast_to(both[None], (fan, 2, HD))


def final_kernel(rows, own_ref, r1, r2, r3, r4, kv_ref, kgain_ref, cos_ref, sin_ref, dk_ref, dv_ref):
    total = own_ref[...]
    for part in (r1, r2, r3, r4):
        total = total + part[...].astype(jnp.float32)
    dv_ref[...] = total[:, HD:].astype(jnp.bfloat16)
    normed, inv = normed_of(kv_ref[:, :HD])
    gained = unrope(total[:, :HD], cos_ref[0:rows, :], sin_ref[0:rows, :]) * kgain_ref[...]
    mean = jnp.mean(gained * normed, axis=-1, keepdims=True)
    dk_ref[...] = ((gained - normed * mean) * inv).astype(jnp.bfloat16)


VMEM = pl.BlockSpec(memory_space=pltpu.VMEM)
SMEM = pl.BlockSpec(memory_space=pltpu.SMEM)
LIMIT = pltpu.CompilerParams(vmem_limit_bytes=40 * 1024 * 1024)


def prepare(doc_lengths, first, rows):
    docs = doc_lengths.shape[1]
    half = jnp.exp(jnp.arange(HALF, dtype=jnp.float32) * (-2.0 * math.log(ROPE_BASE) / HD))
    freq = jnp.concatenate([half, half])[None]
    tab_c, tab_s = rope_tables(rows)
    table = jax.ShapeDtypeStruct((BLOCKS * rows, HD), jnp.float32)
    return pl.pallas_call(
        functools.partial(prep_kernel, rows, docs),
        in_specs=[SMEM, SMEM, VMEM, VMEM, VMEM],
        out_specs=[VMEM, VMEM, VMEM, SMEM],
        out_shape=[
            table,
            table,
            jax.ShapeDtypeStruct((8, rows), jnp.int32),
            jax.ShapeDtypeStruct((2,), jnp.int32),
        ],
        compiler_params=LIMIT,
        name="prep",
    )(doc_lengths, first, freq, tab_c, tab_s)


def attention(scal, low, cos, sin, q_gain, k_gain, window, queries, grads, fan):
    rows, width = queries.shape
    step_width = HEADS_PER_STEP * HD
    by_head = pl.BlockSpec((rows, step_width), lambda i: (0, i))
    size = BLOCKS * rows
    part = jax.ShapeDtypeStruct((rows, 2 * HD), jnp.bfloat16)
    return pl.pallas_call(
        functools.partial(main_kernel, rows, fan),
        grid=(width // step_width,),
        in_specs=[SMEM] + [VMEM] * (5 + BLOCKS) + [by_head, by_head],
        out_specs=[by_head] + [VMEM] * (BLOCKS + 1),
        out_shape=[
            jax.ShapeDtypeStruct((rows, width), jnp.bfloat16),
            jax.ShapeDtypeStruct((rows, 2 * HD), jnp.float32),
            part, part, part, part,
            jax.ShapeDtypeStruct((fan, 2, HD), jnp.float32),
        ],
        scratch_shapes=[
            pltpu.VMEM((size, HD), jnp.bfloat16),
            pltpu.VMEM((size, HD), jnp.bfloat16),
            pltpu.VMEM((size, HD), jnp.float32),
            pltpu.VMEM((size, rows), jnp.float32),
            pltpu.VMEM((size, HD), jnp.float32),
            pltpu.VMEM((size, HD), jnp.float32),
            pltpu.VMEM((8, HD), jnp.float32),
        ],
        compiler_params=LIMIT,
        name="attention",
    )(scal, low, cos, sin, q_gain, k_gain, *window, queries, grads)


def finish(own, parts, kv, k_gain, cos, sin):
    rows = kv.shape[0]
    out = jax.ShapeDtypeStruct((rows, HD), jnp.bfloat16)
    return pl.pallas_call(
        functools.partial(final_kernel, rows),
        in_specs=[VMEM] * 9,
        out_specs=[VMEM, VMEM],
        out_shape=[out, out],
        compiler_params=LIMIT,
        name="finish",
    )(own, *parts, kv, k_gain, cos, sin)


CTX = ("y", "zh")
FAR = ("zl", "c", "zh", "x")


def shifted(block, distance):
    count = lax.axis_size("y") * lax.axis_size("zh")
    return lax.ppermute(block, CTX, [(i, (i + distance) % count) for i in range(count)])


def exchanged(copies, axes):
    return jnp.sum(lax.all_to_all(copies, axes, 0, 0), axis=0)


def on_device(queries_raw, keys_raw, values, grad_out, q_gain, k_gain, doc_lengths):
    rows = queries_raw.shape[1]
    fan = math.prod(lax.axis_size(a) for a in FAR)
    near = lax.axis_size("y")
    ctx_count = near * lax.axis_size("zh")
    shard = lax.axis_index("y") * lax.axis_size("zh") + lax.axis_index("zh")
    kv = jnp.concatenate([keys_raw[0], values[0]], axis=1)
    order = (4, 1, 3, 2)
    got = {d: shifted(kv, d) for d in order}
    first = (shard * rows).astype(jnp.int32).reshape(1)
    cos, sin, low, scal = prepare(doc_lengths, first, rows)
    q_gain2, k_gain2 = q_gain[None], k_gain[None]
    window = [kv] + [got[d] for d in range(1, BLOCKS)]
    dq, own, *terms, gains = attention(
        scal, low, cos, sin, q_gain2, k_gain2, window, queries_raw[0], grad_out[0], fan
    )
    back = {d: shifted(terms[d - 1], -d) for d in order}
    gains = exchanged(gains, FAR)
    gains = exchanged(jnp.broadcast_to(gains[None], (near,) + gains.shape), ("y",))
    loss_scale = (lax.axis_size("zl") * lax.axis_size("c") * ctx_count * rows) ** (-0.5)
    dk, dv = finish(own, [back[d] for d in range(1, BLOCKS)], kv, k_gain2, cos, sin)
    return (dq[None], dk[None], dv[None], gains * loss_scale)


def solution(mesh):
    fine = Mesh(mesh.devices.reshape(2, 2, 8, 4, 4), ("zl", "c", "y", "zh", "x"))
    split = P(("zl", "c"), ("y", "zh"), "x")
    return jax.shard_map(
        on_device,
        mesh=fine,
        in_specs=(split, split, split, split, P(), P(), P(("zl", "c"), None)),
        out_specs=(split, split, split, P()),
        check_vma=False,
    )
```

```python
import functools
import math

import jax
import jax.numpy as jnp
from jax import lax
from jax.experimental import pallas as pl
from jax.experimental.pallas import tpu as pltpu
from jax.sharding import Mesh
from jax.sharding import PartitionSpec as P

REACH = 4
EPSILON = 1e-06
ROPE_BASE = 1000000.0
HD = 128
HALF = HD // 2
BLOCKS = REACH + 1
CHUNK = 128
GROUP = 2
UNROLL = 1
MASKED = -1e30
LOG2E = 1.4426950408889634
SCALE = HD ** (-0.5)
ACROSS = (((1,), (1,)), ((), ()))
ALONG = (((0,), (0,)), ((), ()))


def chunk_rows(i):
    return slice(i * CHUNK, (i + 1) * CHUNK)


def normed_of(source):
    values32 = source.astype(jnp.float32)
    inv = lax.rsqrt(jnp.mean(values32 * values32, axis=-1, keepdims=True) + EPSILON)
    return values32 * inv, inv


def rope(scaled, cos, sin):
    return scaled * cos + pltpu.roll(scaled, HALF, 1) * sin


def unrope(grad, cos, sin):
    return grad * cos - pltpu.roll(grad, HALF, 1) * sin


def fold(terms):
    return jnp.sum(terms.reshape(terms.shape[0] // 8, 8, terms.shape[1]), axis=0)


def fold_max(terms):
    return jnp.max(terms.reshape(terms.shape[0] // 8, 8, terms.shape[1]), axis=0)


def prep_kernel(
    rows, docs, first_ref, lens_ref, gains_ref, q_ref, kv_ref,
    cos_ref, sin_ref, bias_ref, qrot_ref, qnorm_ref, qinv_ref, krot_ref, knorm_ref, gain_ref, scal_ref,
):
    first = first_ref[0]
    chunks = rows // CHUNK
    heads = q_ref.shape[1] // HD
    tok_row = lax.broadcasted_iota(jnp.int32, (8, rows), 1)
    lane = lax.broadcasted_iota(jnp.int32, (8, HD), 1)
    row8 = lax.broadcasted_iota(jnp.int32, (8, HD), 0)
    sign = jnp.where(lane[0:1] < HALF, -1.0, 1.0).astype(jnp.float32)
    half_lane = jnp.where(lane < HALF, lane, lane - HALF).astype(jnp.float32)
    freq = jnp.exp(half_lane * (-2.0 * math.log(ROPE_BASE) / HD))[0:1]
    within = lax.broadcasted_iota(jnp.int32, (CHUNK, HD), 0).astype(jnp.float32) * freq
    within_c, within_s = jnp.cos(within), jnp.sin(within)

    def one_doc(d, carry):
        start, reaching, row = carry
        rel = start - first
        start = start + lens_ref[0, d]
        reaching = jnp.where(rel <= 0, rel, reaching)
        row = jnp.where(tok_row >= rel, rel, row)
        return start, reaching, row

    zero = jnp.int32(0)
    _, reaching, low = lax.fori_loop(0, docs, one_doc, (zero, zero, jnp.zeros((8, rows), jnp.int32)))
    before = -reaching
    scal_ref[0] = 1 + (before + rows - 1) // rows
    position = (tok_row - low).astype(jnp.float32)
    columns = [jnp.broadcast_to(position[0:1, chunk_rows(c)], (CHUNK, CHUNK)).T for c in range(chunks)]
    angles = jnp.where(lane[0:1] < HALF, columns[0], columns[1]) * freq
    packed_c, packed_s = jnp.cos(angles), jnp.sin(angles)
    rolled_c, rolled_s = pltpu.roll(packed_c, HALF, 1), pltpu.roll(packed_s, HALF, 1)
    low_lane = lane[0:1] < HALF
    cos = jnp.concatenate([jnp.where(low_lane, packed_c, rolled_c), jnp.where(low_lane, rolled_c, packed_c)], axis=0)
    sin = jnp.concatenate([jnp.where(low_lane, packed_s, rolled_s), jnp.where(low_lane, rolled_s, packed_s)], axis=0)
    sin = sin * sign
    cos_ref[0:rows, :] = cos
    sin_ref[0:rows, :] = sin
    base = (before - rows * (row8 // chunks + 1) + CHUNK * (row8 % chunks)).astype(jnp.float32) * freq
    base_c, base_s = jnp.cos(base), jnp.sin(base)
    for j in range(chunks * REACH):
        at = chunk_rows(chunks + j)
        c, s = base_c[j : j + 1], base_s[j : j + 1]
        cos_ref[at, :] = c * within_c - s * within_s
        sin_ref[at, :] = (s * within_c + c * within_s) * sign
    key = lax.broadcasted_iota(jnp.int32, (CHUNK, rows), 0)
    tok = lax.broadcasted_iota(jnp.int32, (CHUNK, rows), 1)
    for i in range(chunks + chunks * REACH):
        offset = i % chunks * CHUNK - i // chunks * rows
        kept = key + offset >= low[0:1, :]
        if i < chunks:
            kept = kept & (key + offset <= tok)
        bias_ref[chunk_rows(i), :] = jnp.where(kept, 0.0, MASKED)
    gain_ref[...] = gains_ref[...]
    q_gain, k_gain = gains_ref[0:1], gains_ref[1:2]
    normed, _ = normed_of(kv_ref[:, :HD])
    knorm_ref[...] = normed
    krot_ref[...] = rope(normed * k_gain, cos, sin).astype(jnp.bfloat16)
    for h in range(heads):
        normed, inv = normed_of(q_ref[:, h * HD : (h + 1) * HD])
        qnorm_ref[h] = normed
        qinv_ref[h] = jnp.broadcast_to(inv, (rows, HD))
        qrot_ref[h] = rope(normed * q_gain, cos, sin).astype(jnp.bfloat16)


def main_kernel(
    rows,
    scal_ref, cos_ref, sin_ref, bias_ref, qrot_ref, qnorm_ref, qinv_ref, krot0_ref, knorm0_ref,
    gain_ref, g_ref, w4, w1, w3, w2, w0,
    dq_ref, own_ref, o1, o2, o3, o4, sums_ref,
    krot, vwin, knorm, dk, dv, sums,
):
    heads = qrot_ref.shape[0]
    window = (w0, w1, w2, w3, w4)
    outs = (own_ref, o1, o2, o3, o4)
    q_gain, k_gain = gain_ref[0:1], gain_ref[1:2]
    count = scal_ref[0]
    sums[...] = jnp.zeros_like(sums)
    krot[0:rows, :] = krot0_ref[...]
    knorm[0:rows, :] = knorm0_ref[...]

    def block_rows(d):
        return slice(d * rows, (d + 1) * rows)

    def block_start(d):
        at = block_rows(d)
        vwin[at, :] = window[d][:, HD:]
        dk[at, :] = jnp.zeros((rows, HD), jnp.float32)
        dv[at, :] = jnp.zeros((rows, HD), jnp.float32)
        if d > 0:
            normed, _ = normed_of(window[d][:, :HD])
            knorm[at, :] = normed
            krot[at, :] = rope(normed * k_gain, cos_ref[at, :], sin_ref[at, :]).astype(jnp.bfloat16)

    block_start(0)
    for d in range(1, BLOCKS):
        pl.when(d < count)(functools.partial(block_start, d))

    def attend_group(first, blocks):
        q_rot = qrot_ref[pl.ds(first, GROUP)].reshape(GROUP * rows, HD)
        grad = jnp.concatenate(
            [g_ref[:, pl.ds(pl.multiple_of((first + i) * HD, HD), HD)] for i in range(GROUP)], axis=0
        )
        keys = [chunk_rows(i) for i in range(blocks * rows // CHUNK)]
        scores, wgrads, top = [], [], None
        for at in keys:
            mask = jnp.concatenate([bias_ref[at, :]] * GROUP, axis=1)
            part = lax.dot_general(krot[at, :], q_rot, ACROSS, preferred_element_type=jnp.float32) + mask
            scores.append(part)
            top = fold_max(part) if top is None else jnp.maximum(top, fold_max(part))
        top = jnp.max(top, axis=0, keepdims=True)
        powers, total, dot = [], 0.0, 0.0
        for at, part in zip(keys, scores):
            wgrad = lax.dot_general(vwin[at, :], grad, ACROSS, preferred_element_type=jnp.float32)
            power = jnp.exp2((part - top) * (SCALE * LOG2E))
            total = total + fold(power)
            dot = dot + fold(power * wgrad)
            powers.append(power)
            wgrads.append(wgrad)
        inv_sum = 1.0 / jnp.sum(total, axis=0, keepdims=True)
        delta = jnp.sum(dot, axis=0, keepdims=True) * inv_sum
        sgrads = []
        for at, power, wgrad in zip(keys, powers, wgrads):
            weights = power * inv_sum
            sgrad = (weights * (wgrad - delta)).astype(jnp.bfloat16)
            dv[at, :] += jnp.dot(weights.astype(jnp.bfloat16), grad, preferred_element_type=jnp.float32)
            dk[at, :] += jnp.dot(sgrad, q_rot, preferred_element_type=jnp.float32)
            sgrads.append(sgrad)
        q_grads = 0.0
        for at, sgrad in zip(keys, sgrads):
            q_grads = q_grads + lax.dot_general(sgrad, krot[at, :], ALONG, preferred_element_type=jnp.float32)
        cos, sin = cos_ref[0:rows, :], sin_ref[0:rows, :]
        for i in range(GROUP):
            h = first + i
            q_normed = qnorm_ref[h]
            norm_grad = unrope(q_grads[i * rows : (i + 1) * rows] * SCALE, cos, sin)
            sums[0:8, :] += fold(norm_grad * q_normed)
            gained = norm_grad * q_gain
            mean = jnp.mean(gained * q_normed, axis=-1, keepdims=True)
            dq_ref[:, pl.ds(pl.multiple_of(h * HD, HD), HD)] = ((gained - q_normed * mean) * qinv_ref[h]).astype(jnp.bfloat16)

    def attend(blocks):
        @pl.loop(0, heads // (GROUP * UNROLL))
        def _(j):
            for u in range(UNROLL):
                attend_group((j * UNROLL + u) * GROUP, blocks)

    for blocks in range(1, BLOCKS + 1):
        pl.when(count == blocks)(functools.partial(attend, blocks))

    def block_end(d):
        at = block_rows(d)
        key_grad = dk[at, :] * SCALE
        outs[d][:, :HD] = key_grad.astype(outs[d].dtype)
        outs[d][:, HD:] = dv[at, :].astype(outs[d].dtype)
        norm_grad = unrope(key_grad, cos_ref[at, :], sin_ref[at, :])
        sums[8:16, :] += fold(norm_grad * knorm[at, :])

    def block_unused(d):
        outs[d][...] = jnp.zeros_like(outs[d])

    block_end(0)
    for d in range(1, BLOCKS):
        pl.when(d < count)(functools.partial(block_end, d))
        pl.when(d >= count)(functools.partial(block_unused, d))
    q_sum = jnp.sum(sums[0:8, :], axis=0, keepdims=True)
    k_sum = jnp.sum(sums[8:16, :], axis=0, keepdims=True)
    both = jnp.concatenate([q_sum, k_sum], axis=0)
    sums_ref[...] = jnp.broadcast_to(both[None], sums_ref.shape)


def final_kernel(rows, own_ref, r1, r2, r3, r4, kv_ref, gain_ref, cos_ref, sin_ref, dk_ref, dv_ref):
    total = own_ref[...]
    for part in (r1, r2, r3, r4):
        total = total + part[...].astype(jnp.float32)
    dv_ref[...] = total[:, HD:].astype(jnp.bfloat16)
    normed, inv = normed_of(kv_ref[:, :HD])
    gained = unrope(total[:, :HD], cos_ref[0:rows, :], sin_ref[0:rows, :]) * gain_ref[1:2]
    mean = jnp.mean(gained * normed, axis=-1, keepdims=True)
    dk_ref[...] = ((gained - normed * mean) * inv).astype(jnp.bfloat16)


VMEM = pl.BlockSpec(memory_space=pltpu.VMEM)
SMEM = pl.BlockSpec(memory_space=pltpu.SMEM)
F32 = functools.partial(jax.ShapeDtypeStruct, dtype=jnp.float32)
BF16 = functools.partial(jax.ShapeDtypeStruct, dtype=jnp.bfloat16)
I32 = functools.partial(jax.ShapeDtypeStruct, dtype=jnp.int32)


def limit(mib):
    return pltpu.CompilerParams(vmem_limit_bytes=mib * 1024 * 1024)


def prepare(doc_lengths, first, gains, queries, kv):
    docs = doc_lengths.shape[1]
    rows, width = queries.shape
    heads = width // HD
    size = BLOCKS * rows
    return pl.pallas_call(
        functools.partial(prep_kernel, rows, docs),
        in_specs=[SMEM, SMEM] + [VMEM] * 3,
        out_specs=[VMEM] * 9 + [SMEM],
        out_shape=[
            F32((size, HD)), F32((size, HD)), F32((size, rows)),
            BF16((heads, rows, HD)), F32((heads, rows, HD)), F32((heads, rows, HD)),
            BF16((rows, HD)), F32((rows, HD)), F32((2, HD)),
            I32((1,)),
        ],
        compiler_params=limit(24),
        name="prep",
    )(first, doc_lengths, gains, queries, kv)


def attention(prepared, grads, window, fan):
    *tables, scal = prepared
    rows, width = grads.shape
    size = BLOCKS * rows
    return pl.pallas_call(
        functools.partial(main_kernel, rows),
        in_specs=[SMEM] + [VMEM] * (len(tables) + 1 + BLOCKS),
        out_specs=[VMEM] * (BLOCKS + 2),
        out_shape=[BF16((rows, width)), F32((rows, 2 * HD))] + [BF16((rows, 2 * HD))] * REACH + [F32((fan, 2, HD))],
        scratch_shapes=[
            pltpu.VMEM((size, HD), jnp.bfloat16),
            pltpu.VMEM((size, HD), jnp.bfloat16),
            pltpu.VMEM((size, HD), jnp.float32),
            pltpu.VMEM((size, HD), jnp.float32),
            pltpu.VMEM((size, HD), jnp.float32),
            pltpu.VMEM((16, HD), jnp.float32),
        ],
        compiler_params=limit(32),
        name="attention",
    )(scal, *tables, grads, window[4], window[1], window[3], window[2], window[0])


def finish(own, parts, kv, prepared):
    rows = kv.shape[0]
    return pl.pallas_call(
        functools.partial(final_kernel, rows),
        in_specs=[VMEM] * 9,
        out_specs=[VMEM, VMEM],
        out_shape=[BF16((rows, HD)), BF16((rows, HD))],
        compiler_params=limit(16),
        name="finish",
    )(own, *parts, kv, prepared[8], prepared[0], prepared[1])


CTX = ("y", "zh")
FAR = ("zl", "c", "zh", "x")


def shifted(block, distance):
    count = lax.axis_size("y") * lax.axis_size("zh")
    return lax.ppermute(block, CTX, [(i, (i + distance) % count) for i in range(count)])


def exchanged(copies, axes):
    return jnp.sum(lax.all_to_all(copies, axes, 0, 0), axis=0)


def on_device(queries_raw, keys_raw, values, grad_out, q_gain, k_gain, doc_lengths):
    rows = queries_raw.shape[1]
    fan = math.prod(lax.axis_size(a) for a in FAR)
    near = lax.axis_size("y")
    ctx_count = near * lax.axis_size("zh")
    shard = lax.axis_index("y") * lax.axis_size("zh") + lax.axis_index("zh")
    kv = jnp.concatenate([keys_raw[0], values[0]], axis=1)
    got = {d: shifted(kv, d) for d in (2, 3, 1, 4)}
    first = (shard * rows).astype(jnp.int32).reshape(1)
    prepared = prepare(doc_lengths, first, jnp.stack([q_gain, k_gain]), queries_raw[0], kv)
    window = [kv] + [got[d] for d in range(1, BLOCKS)]
    dq, own, *terms, gains = attention(prepared, grad_out[0], window, fan)
    back = {d: shifted(terms[d - 1], -d) for d in (2, 3, 1, 4)}
    gains = exchanged(gains, FAR)
    gains = exchanged(jnp.broadcast_to(gains[None], (near,) + gains.shape), ("y",))
    loss_scale = (lax.axis_size("zl") * lax.axis_size("c") * ctx_count * rows) ** (-0.5)
    dk, dv = finish(own, [back[d] for d in range(1, BLOCKS)], kv, prepared)
    return (dq[None], dk[None], dv[None], gains * loss_scale)


def solution(mesh):
    fine = Mesh(mesh.devices.reshape(2, 2, 8, 4, 4), ("zl", "c", "y", "zh", "x"))
    split = P(("zl", "c"), ("y", "zh"), "x")
    return jax.shard_map(
        on_device,
        mesh=fine,
        in_specs=(split, split, split, split, P(), P(), P(("zl", "c"), None)),
        out_specs=(split, split, split, P()),
        check_vma=False,
    )
```

```python
import functools
import math

import jax
import jax.numpy as jnp
from jax import lax
from jax.experimental import pallas as pl
from jax.experimental.pallas import tpu as pltpu
from jax.sharding import Mesh
from jax.sharding import PartitionSpec as P

REACH = 4
EPSILON = 1e-06
ROPE_BASE = 1000000.0
HD = 128
HALF = HD // 2
BLOCKS = REACH + 1
CHUNK = 128
GROUP = 2
UNROLL = 2
LAG = 1
MASKED = -1e30
LOG2E = 1.4426950408889634
SCALE = HD ** (-0.5)
ACROSS = (((1,), (1,)), ((), ()))
ALONG = (((0,), (0,)), ((), ()))


def chunk_rows(i):
    return slice(i * CHUNK, (i + 1) * CHUNK)


def normed_of(source):
    values32 = source.astype(jnp.float32)
    inv = lax.rsqrt(jnp.mean(values32 * values32, axis=-1, keepdims=True) + EPSILON)
    return values32 * inv, inv


def rope(scaled, cos, sin):
    return scaled * cos + pltpu.roll(scaled, HALF, 1) * sin


def unrope(grad, cos, sin):
    return grad * cos - pltpu.roll(grad, HALF, 1) * sin


def fold(terms):
    return jnp.sum(terms.reshape(terms.shape[0] // 8, 8, terms.shape[1]), axis=0)


def fold_max(terms):
    return jnp.max(terms.reshape(terms.shape[0] // 8, 8, terms.shape[1]), axis=0)


def prep_kernel(
    rows, docs, first_ref, lens_ref, gains_ref, q_ref, kv_ref,
    cos_ref, sin_ref, bias_ref, qrot_ref, qnorm_ref, qinv_ref, krot_ref, knorm_ref, gain_ref, scal_ref,
):
    first = first_ref[0]
    chunks = rows // CHUNK
    heads = q_ref.shape[1] // HD
    tok_row = lax.broadcasted_iota(jnp.int32, (8, rows), 1)
    lane = lax.broadcasted_iota(jnp.int32, (8, HD), 1)
    row8 = lax.broadcasted_iota(jnp.int32, (8, HD), 0)
    sign = jnp.where(lane[0:1] < HALF, -1.0, 1.0).astype(jnp.float32)
    half_lane = jnp.where(lane < HALF, lane, lane - HALF).astype(jnp.float32)
    freq = jnp.exp(half_lane * (-2.0 * math.log(ROPE_BASE) / HD))[0:1]
    within = lax.broadcasted_iota(jnp.int32, (CHUNK, HD), 0).astype(jnp.float32) * freq
    within_c, within_s = jnp.cos(within), jnp.sin(within)

    def one_doc(d, carry):
        start, reaching, row = carry
        rel = start - first
        start = start + lens_ref[0, d]
        reaching = jnp.where(rel <= 0, rel, reaching)
        row = jnp.where(tok_row >= rel, rel, row)
        return start, reaching, row

    zero = jnp.int32(0)
    _, reaching, low = lax.fori_loop(0, docs, one_doc, (zero, zero, jnp.zeros((8, rows), jnp.int32)))
    before = -reaching
    scal_ref[0] = 1 + (before + rows - 1) // rows
    position = (tok_row - low).astype(jnp.float32)
    columns = [jnp.broadcast_to(position[0:1, chunk_rows(c)], (CHUNK, CHUNK)).T for c in range(chunks)]
    angles = jnp.where(lane[0:1] < HALF, columns[0], columns[1]) * freq
    packed_c, packed_s = jnp.cos(angles), jnp.sin(angles)
    rolled_c, rolled_s = pltpu.roll(packed_c, HALF, 1), pltpu.roll(packed_s, HALF, 1)
    low_lane = lane[0:1] < HALF
    cos = jnp.concatenate([jnp.where(low_lane, packed_c, rolled_c), jnp.where(low_lane, rolled_c, packed_c)], axis=0)
    sin = jnp.concatenate([jnp.where(low_lane, packed_s, rolled_s), jnp.where(low_lane, rolled_s, packed_s)], axis=0)
    sin = sin * sign
    cos_ref[0:rows, :] = cos
    sin_ref[0:rows, :] = sin
    base = (before - rows * (row8 // chunks + 1) + CHUNK * (row8 % chunks)).astype(jnp.float32) * freq
    base_c, base_s = jnp.cos(base), jnp.sin(base)
    for j in range(chunks * REACH):
        at = chunk_rows(chunks + j)
        c, s = base_c[j : j + 1], base_s[j : j + 1]
        cos_ref[at, :] = c * within_c - s * within_s
        sin_ref[at, :] = (s * within_c + c * within_s) * sign
    key = lax.broadcasted_iota(jnp.int32, (CHUNK, rows), 0)
    tok = lax.broadcasted_iota(jnp.int32, (CHUNK, rows), 1)
    for i in range(chunks + chunks * REACH):
        offset = i % chunks * CHUNK - i // chunks * rows
        kept = key + offset >= low[0:1, :]
        if i < chunks:
            kept = kept & (key + offset <= tok)
        bias_ref[chunk_rows(i), :] = jnp.where(kept, 0.0, MASKED)
    gain_ref[...] = gains_ref[...]
    q_gain, k_gain = gains_ref[0:1], gains_ref[1:2]
    normed, _ = normed_of(kv_ref[:, :HD])
    knorm_ref[...] = normed
    krot_ref[...] = rope(normed * k_gain, cos, sin).astype(jnp.bfloat16)
    for h in range(heads):
        normed, inv = normed_of(q_ref[:, h * HD : (h + 1) * HD])
        qnorm_ref[h] = normed
        qinv_ref[h] = jnp.broadcast_to(inv, (rows, HD))
        qrot_ref[h] = rope(normed * q_gain, cos, sin).astype(jnp.bfloat16)


def main_kernel(
    rows,
    scal_ref, cos_ref, sin_ref, bias_ref, qrot_ref, qnorm_ref, qinv_ref, krot0_ref, knorm0_ref,
    gain_ref, g_ref, w4, w1, w3, w2, w0,
    dq_ref, own_ref, o1, o2, o3, o4, sums_ref,
    krot, vwin, knorm, dk, dv, sums,
):
    heads = qrot_ref.shape[0]
    window = (w0, w1, w2, w3, w4)
    outs = (own_ref, o1, o2, o3, o4)
    q_gain, k_gain = gain_ref[0:1], gain_ref[1:2]
    count = scal_ref[0]
    sums[...] = jnp.zeros_like(sums)
    krot[0:rows, :] = krot0_ref[...]
    knorm[0:rows, :] = knorm0_ref[...]

    def block_rows(d):
        return slice(d * rows, (d + 1) * rows)

    def block_start(d):
        at = block_rows(d)
        vwin[at, :] = window[d][:, HD:]
        dk[at, :] = jnp.zeros((rows, HD), jnp.float32)
        dv[at, :] = jnp.zeros((rows, HD), jnp.float32)
        if d > 0:
            normed, _ = normed_of(window[d][:, :HD])
            knorm[at, :] = normed
            krot[at, :] = rope(normed * k_gain, cos_ref[at, :], sin_ref[at, :]).astype(jnp.bfloat16)

    block_start(0)
    for d in range(1, BLOCKS):
        pl.when(d < count)(functools.partial(block_start, d))

    def attend_group(first, blocks):
        q_rot = qrot_ref[pl.ds(first, GROUP)].reshape(GROUP * rows, HD)
        grad = jnp.concatenate(
            [g_ref[:, pl.ds(pl.multiple_of((first + i) * HD, HD), HD)] for i in range(GROUP)], axis=0
        )
        keys = [chunk_rows(i) for i in range(blocks * rows // CHUNK)]
        scores, wgrads, top = [], [], None
        for at in keys:
            mask = jnp.concatenate([bias_ref[at, :]] * GROUP, axis=1)
            part = lax.dot_general(krot[at, :], q_rot, ACROSS, preferred_element_type=jnp.float32) + mask
            scores.append(part)
            top = fold_max(part) if top is None else jnp.maximum(top, fold_max(part))
            yield
        top = jnp.max(top, axis=0, keepdims=True)
        powers, total, dot = [], 0.0, 0.0
        for at, part in zip(keys, scores):
            wgrad = lax.dot_general(vwin[at, :], grad, ACROSS, preferred_element_type=jnp.float32)
            power = jnp.exp2((part - top) * (SCALE * LOG2E))
            total = total + fold(power)
            dot = dot + fold(power * wgrad)
            powers.append(power)
            wgrads.append(wgrad)
            yield
        inv_sum = 1.0 / jnp.sum(total, axis=0, keepdims=True)
        delta = jnp.sum(dot, axis=0, keepdims=True) * inv_sum
        sgrads = []
        for at, power, wgrad in zip(keys, powers, wgrads):
            weights = power * inv_sum
            sgrad = (weights * (wgrad - delta)).astype(jnp.bfloat16)
            dv[at, :] += jnp.dot(weights.astype(jnp.bfloat16), grad, preferred_element_type=jnp.float32)
            dk[at, :] += jnp.dot(sgrad, q_rot, preferred_element_type=jnp.float32)
            sgrads.append(sgrad)
            yield
        q_grads = 0.0
        for at, sgrad in zip(keys, sgrads):
            q_grads = q_grads + lax.dot_general(sgrad, krot[at, :], ALONG, preferred_element_type=jnp.float32)
        yield
        cos, sin = cos_ref[0:rows, :], sin_ref[0:rows, :]
        for i in range(GROUP):
            h = first + i
            q_normed = qnorm_ref[h]
            norm_grad = unrope(q_grads[i * rows : (i + 1) * rows] * SCALE, cos, sin)
            sums[0:8, :] += fold(norm_grad * q_normed)
            gained = norm_grad * q_gain
            mean = jnp.mean(gained * q_normed, axis=-1, keepdims=True)
            dq_ref[:, pl.ds(pl.multiple_of(h * HD, HD), HD)] = ((gained - q_normed * mean) * qinv_ref[h]).astype(jnp.bfloat16)

    def attend(blocks):
        @pl.loop(0, heads // (GROUP * UNROLL))
        def _(j):
            waiting = [attend_group((j * UNROLL + u) * GROUP, blocks) for u in range(UNROLL)]
            running, tick = [], 0
            lag = max(1, LAG * blocks * rows // CHUNK)
            while waiting or running:
                if waiting and tick % lag == 0:
                    running.append(waiting.pop(0))
                tick += 1
                for group in list(running):
                    if next(group, "end") == "end":
                        running.remove(group)

    for blocks in range(1, BLOCKS + 1):
        pl.when(count == blocks)(functools.partial(attend, blocks))

    def block_end(d):
        at = block_rows(d)
        key_grad = dk[at, :] * SCALE
        outs[d][:, :HD] = key_grad.astype(outs[d].dtype)
        outs[d][:, HD:] = dv[at, :].astype(outs[d].dtype)
        norm_grad = unrope(key_grad, cos_ref[at, :], sin_ref[at, :])
        sums[8:16, :] += fold(norm_grad * knorm[at, :])

    def block_unused(d):
        outs[d][...] = jnp.zeros_like(outs[d])

    block_end(0)
    for d in range(1, BLOCKS):
        pl.when(d < count)(functools.partial(block_end, d))
        pl.when(d >= count)(functools.partial(block_unused, d))
    q_sum = jnp.sum(sums[0:8, :], axis=0, keepdims=True)
    k_sum = jnp.sum(sums[8:16, :], axis=0, keepdims=True)
    both = jnp.concatenate([q_sum, k_sum], axis=0)
    sums_ref[...] = jnp.broadcast_to(both[None], sums_ref.shape)


def final_kernel(rows, own_ref, r1, r2, r3, r4, kv_ref, gain_ref, cos_ref, sin_ref, dk_ref, dv_ref):
    total = own_ref[...]
    for part in (r1, r2, r3, r4):
        total = total + part[...].astype(jnp.float32)
    dv_ref[...] = total[:, HD:].astype(jnp.bfloat16)
    normed, inv = normed_of(kv_ref[:, :HD])
    gained = unrope(total[:, :HD], cos_ref[0:rows, :], sin_ref[0:rows, :]) * gain_ref[1:2]
    mean = jnp.mean(gained * normed, axis=-1, keepdims=True)
    dk_ref[...] = ((gained - normed * mean) * inv).astype(jnp.bfloat16)


VMEM = pl.BlockSpec(memory_space=pltpu.VMEM)
SMEM = pl.BlockSpec(memory_space=pltpu.SMEM)
F32 = functools.partial(jax.ShapeDtypeStruct, dtype=jnp.float32)
BF16 = functools.partial(jax.ShapeDtypeStruct, dtype=jnp.bfloat16)
I32 = functools.partial(jax.ShapeDtypeStruct, dtype=jnp.int32)


def limit(mib):
    return pltpu.CompilerParams(vmem_limit_bytes=mib * 1024 * 1024)


def prepare(doc_lengths, first, gains, queries, kv):
    docs = doc_lengths.shape[1]
    rows, width = queries.shape
    heads = width // HD
    size = BLOCKS * rows
    return pl.pallas_call(
        functools.partial(prep_kernel, rows, docs),
        in_specs=[SMEM, SMEM] + [VMEM] * 3,
        out_specs=[VMEM] * 9 + [SMEM],
        out_shape=[
            F32((size, HD)), F32((size, HD)), F32((size, rows)),
            BF16((heads, rows, HD)), F32((heads, rows, HD)), F32((heads, rows, HD)),
            BF16((rows, HD)), F32((rows, HD)), F32((2, HD)),
            I32((1,)),
        ],
        compiler_params=limit(24),
        name="prep",
    )(first, doc_lengths, gains, queries, kv)


def attention(prepared, grads, window, fan):
    *tables, scal = prepared
    rows, width = grads.shape
    size = BLOCKS * rows
    return pl.pallas_call(
        functools.partial(main_kernel, rows),
        in_specs=[SMEM] + [VMEM] * (len(tables) + 1 + BLOCKS),
        out_specs=[VMEM] * (BLOCKS + 2),
        out_shape=[BF16((rows, width)), F32((rows, 2 * HD))] + [BF16((rows, 2 * HD))] * REACH + [F32((fan, 2, HD))],
        scratch_shapes=[
            pltpu.VMEM((size, HD), jnp.bfloat16),
            pltpu.VMEM((size, HD), jnp.bfloat16),
            pltpu.VMEM((size, HD), jnp.float32),
            pltpu.VMEM((size, HD), jnp.float32),
            pltpu.VMEM((size, HD), jnp.float32),
            pltpu.VMEM((16, HD), jnp.float32),
        ],
        compiler_params=limit(32),
        name="attention",
    )(scal, *tables, grads, window[4], window[1], window[3], window[2], window[0])


def finish(own, parts, kv, prepared):
    rows = kv.shape[0]
    return pl.pallas_call(
        functools.partial(final_kernel, rows),
        in_specs=[VMEM] * 9,
        out_specs=[VMEM, VMEM],
        out_shape=[BF16((rows, HD)), BF16((rows, HD))],
        compiler_params=limit(16),
        name="finish",
    )(own, *parts, kv, prepared[8], prepared[0], prepared[1])


CTX = ("y", "zh")
FAR = ("zl", "c", "zh", "x")


def shifted(block, distance):
    count = lax.axis_size("y") * lax.axis_size("zh")
    return lax.ppermute(block, CTX, [(i, (i + distance) % count) for i in range(count)])


def exchanged(copies, axes):
    return jnp.sum(lax.all_to_all(copies, axes, 0, 0), axis=0)


def on_device(queries_raw, keys_raw, values, grad_out, q_gain, k_gain, doc_lengths):
    rows = queries_raw.shape[1]
    fan = math.prod(lax.axis_size(a) for a in FAR)
    near = lax.axis_size("y")
    ctx_count = near * lax.axis_size("zh")
    shard = lax.axis_index("y") * lax.axis_size("zh") + lax.axis_index("zh")
    kv = jnp.concatenate([keys_raw[0], values[0]], axis=1)
    got = {d: shifted(kv, d) for d in (2, 3, 1, 4)}
    first = (shard * rows).astype(jnp.int32).reshape(1)
    prepared = prepare(doc_lengths, first, jnp.stack([q_gain, k_gain]), queries_raw[0], kv)
    window = [kv] + [got[d] for d in range(1, BLOCKS)]
    dq, own, *terms, gains = attention(prepared, grad_out[0], window, fan)
    back = {d: shifted(terms[d - 1], -d) for d in (2, 3, 1, 4)}
    gains = exchanged(gains, FAR)
    gains = exchanged(jnp.broadcast_to(gains[None], (near,) + gains.shape), ("y",))
    loss_scale = (lax.axis_size("zl") * lax.axis_size("c") * ctx_count * rows) ** (-0.5)
    dk, dv = finish(own, [back[d] for d in range(1, BLOCKS)], kv, prepared)
    return (dq[None], dk[None], dv[None], gains * loss_scale)


def solution(mesh):
    fine = Mesh(mesh.devices.reshape(2, 2, 8, 4, 4), ("zl", "c", "y", "zh", "x"))
    split = P(("zl", "c"), ("y", "zh"), "x")
    return jax.shard_map(
        on_device,
        mesh=fine,
        in_specs=(split, split, split, split, P(), P(), P(("zl", "c"), None)),
        out_specs=(split, split, split, P()),
        check_vma=False,
    )
```

```python
import functools
import math

import jax
import jax.numpy as jnp
from jax import lax
from jax.experimental import pallas as pl
from jax.experimental.pallas import tpu as pltpu
from jax.sharding import Mesh
from jax.sharding import PartitionSpec as P

REACH = 4
EPSILON = 1e-06
ROPE_BASE = 1000000.0
HD = 128
HALF = HD // 2
BLOCKS = REACH + 1
CHUNK = 128
GROUP = 2
UNROLL = 2
LAG = 1
MASKED = -1e30
LOG2E = 1.4426950408889634
SCALE = HD ** (-0.5)
ACROSS = (((1,), (1,)), ((), ()))
ALONG = (((0,), (0,)), ((), ()))


def chunk_rows(i):
    return slice(i * CHUNK, (i + 1) * CHUNK)


def normed_of(source):
    values32 = source.astype(jnp.float32)
    inv = lax.rsqrt(jnp.mean(values32 * values32, axis=-1, keepdims=True) + EPSILON)
    return values32 * inv, inv


def rope(scaled, cos, sin):
    return scaled * cos + pltpu.roll(scaled, HALF, 1) * sin


def unrope(grad, cos, sin):
    return grad * cos - pltpu.roll(grad, HALF, 1) * sin


def fold(terms):
    return jnp.sum(terms.reshape(terms.shape[0] // 8, 8, terms.shape[1]), axis=0)


def fold_max(terms):
    return jnp.max(terms.reshape(terms.shape[0] // 8, 8, terms.shape[1]), axis=0)


def prep_kernel(
    rows, first_ref, packed_ref, q_ref, kv_ref,
    cos_ref, sin_ref, bias_ref, qrot_ref, qnorm_ref, qinv_ref, krot_ref, knorm_ref, gain_ref, scal_ref,
):
    first = first_ref[0]
    chunks = rows // CHUNK
    heads = q_ref.shape[1] // HD
    lane = lax.broadcasted_iota(jnp.int32, (8, HD), 1)
    row8 = lax.broadcasted_iota(jnp.int32, (8, HD), 0)
    sign = jnp.where(lane[0:1] < HALF, -1.0, 1.0).astype(jnp.float32)
    half_lane = jnp.where(lane < HALF, lane, lane - HALF).astype(jnp.float32)
    freq = jnp.exp(half_lane * (-2.0 * math.log(ROPE_BASE) / HD))[0:1]
    within = lax.broadcasted_iota(jnp.int32, (CHUNK, HD), 0).astype(jnp.float32) * freq
    within_c, within_s = jnp.cos(within), jnp.sin(within)

    inner = lax.broadcasted_iota(jnp.int32, (HD, HD), 1) < lax.broadcasted_iota(jnp.int32, (HD, HD), 0)
    starts = jnp.sum(jnp.where(inner, packed_ref[2:3], 0.0), axis=1, keepdims=True)
    rel = starts - first.astype(jnp.float32)
    tok = lax.broadcasted_iota(jnp.int32, (HD, rows), 1).astype(jnp.float32)
    low = jnp.max(jnp.where(rel <= tok, rel, MASKED), axis=0, keepdims=True)
    before = -jnp.max(jnp.where(rel <= 0.0, rel, MASKED))
    count = jnp.int32(1)
    for d in range(REACH):
        count = count + jnp.where(before > float(d * rows), 1, 0)
    scal_ref[0] = count
    position = tok[0:1] - low
    columns = [jnp.broadcast_to(position[:, chunk_rows(c)], (CHUNK, CHUNK)).T for c in range(chunks)]
    angles = jnp.where(lane[0:1] < HALF, columns[0], columns[1]) * freq
    packed_c, packed_s = jnp.cos(angles), jnp.sin(angles)
    rolled_c, rolled_s = pltpu.roll(packed_c, HALF, 1), pltpu.roll(packed_s, HALF, 1)
    low_lane = lane[0:1] < HALF
    cos = jnp.concatenate([jnp.where(low_lane, packed_c, rolled_c), jnp.where(low_lane, rolled_c, packed_c)], axis=0)
    sin = jnp.concatenate([jnp.where(low_lane, packed_s, rolled_s), jnp.where(low_lane, rolled_s, packed_s)], axis=0)
    sin = sin * sign
    cos_ref[0:rows, :] = cos
    sin_ref[0:rows, :] = sin
    base = (before + (CHUNK * (row8 % chunks) - rows * (row8 // chunks + 1)).astype(jnp.float32)) * freq
    base_c, base_s = jnp.cos(base), jnp.sin(base)
    for j in range(chunks * REACH):
        at = chunk_rows(chunks + j)
        c, s = base_c[j : j + 1], base_s[j : j + 1]
        cos_ref[at, :] = c * within_c - s * within_s
        sin_ref[at, :] = (s * within_c + c * within_s) * sign
    key = lax.broadcasted_iota(jnp.int32, (CHUNK, rows), 0)
    tok = lax.broadcasted_iota(jnp.int32, (CHUNK, rows), 1)
    low = low.astype(jnp.int32)
    for i in range(chunks + chunks * REACH):
        offset = i % chunks * CHUNK - i // chunks * rows
        kept = key + offset >= low
        if i < chunks:
            kept = kept & (key + offset <= tok)
        bias_ref[chunk_rows(i), :] = jnp.where(kept, 0.0, MASKED)
    gain_ref[...] = packed_ref[0:2]
    q_gain, k_gain = packed_ref[0:1], packed_ref[1:2]
    normed, _ = normed_of(kv_ref[:, :HD])
    knorm_ref[...] = normed
    krot_ref[...] = rope(normed * k_gain, cos, sin).astype(jnp.bfloat16)
    for h in range(heads):
        normed, inv = normed_of(q_ref[:, h * HD : (h + 1) * HD])
        qnorm_ref[h] = normed
        qinv_ref[h] = jnp.broadcast_to(inv, (rows, HD))
        qrot_ref[h] = rope(normed * q_gain, cos, sin).astype(jnp.bfloat16)


def main_kernel(
    rows,
    scal_ref, cos_ref, sin_ref, bias_ref, qrot_ref, qnorm_ref, qinv_ref, krot0_ref, knorm0_ref,
    gain_ref, g_ref, w4, w1, w3, w2, w0,
    dq_ref, own_ref, o1, o2, o3, o4, sums_ref,
    krot, vwin, knorm, dk, dv, sums,
):
    heads = qrot_ref.shape[0]
    window = (w0, w1, w2, w3, w4)
    outs = (own_ref, o1, o2, o3, o4)
    q_gain, k_gain = gain_ref[0:1], gain_ref[1:2]
    count = scal_ref[0]
    sums[...] = jnp.zeros_like(sums)
    krot[0:rows, :] = krot0_ref[...]
    knorm[0:rows, :] = knorm0_ref[...]

    def block_rows(d):
        return slice(d * rows, (d + 1) * rows)

    def block_start(d):
        at = block_rows(d)
        vwin[at, :] = window[d][:, HD:]
        dk[at, :] = jnp.zeros((rows, HD), jnp.float32)
        dv[at, :] = jnp.zeros((rows, HD), jnp.float32)
        if d > 0:
            normed, _ = normed_of(window[d][:, :HD])
            knorm[at, :] = normed
            krot[at, :] = rope(normed * k_gain, cos_ref[at, :], sin_ref[at, :]).astype(jnp.bfloat16)

    block_start(0)
    for d in range(1, BLOCKS):
        pl.when(d < count)(functools.partial(block_start, d))

    def attend_group(first, blocks):
        q_rot = qrot_ref[pl.ds(first, GROUP)].reshape(GROUP * rows, HD)
        grad = jnp.concatenate(
            [g_ref[:, pl.ds(pl.multiple_of((first + i) * HD, HD), HD)] for i in range(GROUP)], axis=0
        )
        keys = [chunk_rows(i) for i in range(blocks * rows // CHUNK)]
        scores, wgrads, top = [], [], None
        for at in keys:
            mask = jnp.concatenate([bias_ref[at, :]] * GROUP, axis=1)
            part = lax.dot_general(krot[at, :], q_rot, ACROSS, preferred_element_type=jnp.float32) + mask
            scores.append(part)
            top = fold_max(part) if top is None else jnp.maximum(top, fold_max(part))
            yield
        top = jnp.max(top, axis=0, keepdims=True)
        powers, total, dot = [], 0.0, 0.0
        for at, part in zip(keys, scores):
            wgrad = lax.dot_general(vwin[at, :], grad, ACROSS, preferred_element_type=jnp.float32)
            power = jnp.exp2((part - top) * (SCALE * LOG2E))
            total = total + fold(power)
            dot = dot + fold(power * wgrad)
            powers.append(power)
            wgrads.append(wgrad)
            yield
        inv_sum = 1.0 / jnp.sum(total, axis=0, keepdims=True)
        delta = jnp.sum(dot, axis=0, keepdims=True) * inv_sum
        sgrads = []
        for at, power, wgrad in zip(keys, powers, wgrads):
            weights = power * inv_sum
            sgrad = (weights * (wgrad - delta)).astype(jnp.bfloat16)
            dv[at, :] += jnp.dot(weights.astype(jnp.bfloat16), grad, preferred_element_type=jnp.float32)
            dk[at, :] += jnp.dot(sgrad, q_rot, preferred_element_type=jnp.float32)
            sgrads.append(sgrad)
            yield
        q_grads = 0.0
        for at, sgrad in zip(keys, sgrads):
            q_grads = q_grads + lax.dot_general(sgrad, krot[at, :], ALONG, preferred_element_type=jnp.float32)
        yield
        cos, sin = cos_ref[0:rows, :], sin_ref[0:rows, :]
        for i in range(GROUP):
            h = first + i
            q_normed = qnorm_ref[h]
            norm_grad = unrope(q_grads[i * rows : (i + 1) * rows] * SCALE, cos, sin)
            sums[0:8, :] += fold(norm_grad * q_normed)
            gained = norm_grad * q_gain
            mean = jnp.mean(gained * q_normed, axis=-1, keepdims=True)
            dq_ref[:, pl.ds(pl.multiple_of(h * HD, HD), HD)] = ((gained - q_normed * mean) * qinv_ref[h]).astype(jnp.bfloat16)

    def attend(blocks):
        @pl.loop(0, heads // (GROUP * UNROLL))
        def _(j):
            waiting = [attend_group((j * UNROLL + u) * GROUP, blocks) for u in range(UNROLL)]
            running, tick = [], 0
            lag = max(1, LAG * blocks * rows // CHUNK)
            while waiting or running:
                if waiting and tick % lag == 0:
                    running.append(waiting.pop(0))
                tick += 1
                for group in list(running):
                    if next(group, "end") == "end":
                        running.remove(group)

    for blocks in range(1, BLOCKS + 1):
        pl.when(count == blocks)(functools.partial(attend, blocks))

    def block_end(d):
        at = block_rows(d)
        key_grad = dk[at, :] * SCALE
        outs[d][:, :HD] = key_grad.astype(outs[d].dtype)
        outs[d][:, HD:] = dv[at, :].astype(outs[d].dtype)
        norm_grad = unrope(key_grad, cos_ref[at, :], sin_ref[at, :])
        sums[8:16, :] += fold(norm_grad * knorm[at, :])

    def block_unused(d):
        outs[d][...] = jnp.zeros_like(outs[d])

    block_end(0)
    for d in range(1, BLOCKS):
        pl.when(d < count)(functools.partial(block_end, d))
        pl.when(d >= count)(functools.partial(block_unused, d))
    q_sum = jnp.sum(sums[0:8, :], axis=0, keepdims=True)
    k_sum = jnp.sum(sums[8:16, :], axis=0, keepdims=True)
    both = jnp.concatenate([q_sum, k_sum], axis=0)
    sums_ref[...] = jnp.broadcast_to(both[None], sums_ref.shape)


def final_kernel(rows, own_ref, r1, r2, r3, r4, kv_ref, gain_ref, cos_ref, sin_ref, dk_ref, dv_ref):
    total = own_ref[...]
    for part in (r1, r2, r3, r4):
        total = total + part[...].astype(jnp.float32)
    dv_ref[...] = total[:, HD:].astype(jnp.bfloat16)
    normed, inv = normed_of(kv_ref[:, :HD])
    gained = unrope(total[:, :HD], cos_ref[0:rows, :], sin_ref[0:rows, :]) * gain_ref[1:2]
    mean = jnp.mean(gained * normed, axis=-1, keepdims=True)
    dk_ref[...] = ((gained - normed * mean) * inv).astype(jnp.bfloat16)


VMEM = pl.BlockSpec(memory_space=pltpu.VMEM)
SMEM = pl.BlockSpec(memory_space=pltpu.SMEM)
F32 = functools.partial(jax.ShapeDtypeStruct, dtype=jnp.float32)
BF16 = functools.partial(jax.ShapeDtypeStruct, dtype=jnp.bfloat16)
I32 = functools.partial(jax.ShapeDtypeStruct, dtype=jnp.int32)


def limit(mib):
    return pltpu.CompilerParams(vmem_limit_bytes=mib * 1024 * 1024)


def prepare(first, packed, queries, kv):
    rows, width = queries.shape
    heads = width // HD
    size = BLOCKS * rows
    return pl.pallas_call(
        functools.partial(prep_kernel, rows),
        in_specs=[SMEM] + [VMEM] * 3,
        out_specs=[VMEM] * 9 + [SMEM],
        out_shape=[
            F32((size, HD)), F32((size, HD)), F32((size, rows)),
            BF16((heads, rows, HD)), F32((heads, rows, HD)), F32((heads, rows, HD)),
            BF16((rows, HD)), F32((rows, HD)), F32((2, HD)),
            I32((1,)),
        ],
        compiler_params=limit(24),
        name="prep",
    )(first, packed, queries, kv)


def attention(prepared, grads, window, fan):
    *tables, scal = prepared
    rows, width = grads.shape
    size = BLOCKS * rows
    return pl.pallas_call(
        functools.partial(main_kernel, rows),
        in_specs=[SMEM] + [VMEM] * (len(tables) + 1 + BLOCKS),
        out_specs=[VMEM] * (BLOCKS + 2),
        out_shape=[BF16((rows, width)), F32((rows, 2 * HD))] + [BF16((rows, 2 * HD))] * REACH + [F32((fan, 2, HD))],
        scratch_shapes=[
            pltpu.VMEM((size, HD), jnp.bfloat16),
            pltpu.VMEM((size, HD), jnp.bfloat16),
            pltpu.VMEM((size, HD), jnp.float32),
            pltpu.VMEM((size, HD), jnp.float32),
            pltpu.VMEM((size, HD), jnp.float32),
            pltpu.VMEM((16, HD), jnp.float32),
        ],
        compiler_params=limit(32),
        name="attention",
    )(scal, *tables, grads, window[4], window[1], window[3], window[2], window[0])


def finish(own, parts, kv, prepared):
    rows = kv.shape[0]
    return pl.pallas_call(
        functools.partial(final_kernel, rows),
        in_specs=[VMEM] * 9,
        out_specs=[VMEM, VMEM],
        out_shape=[BF16((rows, HD)), BF16((rows, HD))],
        compiler_params=limit(16),
        name="finish",
    )(own, *parts, kv, prepared[8], prepared[0], prepared[1])


CTX = ("y", "zh")
FAR = ("zl", "c", "zh", "x")


def shifted(block, distance):
    count = lax.axis_size("y") * lax.axis_size("zh")
    return lax.ppermute(block, CTX, [(i, (i + distance) % count) for i in range(count)])


def exchanged(copies, axes):
    return jnp.sum(lax.all_to_all(copies, axes, 0, 0), axis=0)


def on_device(queries_raw, keys_raw, values, grad_out, q_gain, k_gain, doc_lengths):
    rows = queries_raw.shape[1]
    fan = math.prod(lax.axis_size(a) for a in FAR)
    near = lax.axis_size("y")
    ctx_count = near * lax.axis_size("zh")
    shard = lax.axis_index("y") * lax.axis_size("zh") + lax.axis_index("zh")
    kv = jnp.concatenate([keys_raw[0], values[0]], axis=1)
    got = {d: shifted(kv, d) for d in (2, 3, 1, 4)}
    first = (shard * rows).astype(jnp.int32).reshape(1)
    lengths = jnp.pad(doc_lengths[0].astype(jnp.float32), (0, HD - doc_lengths.shape[1]))
    prepared = prepare(first, jnp.stack([q_gain, k_gain, lengths]), queries_raw[0], kv)
    window = [kv] + [got[d] for d in range(1, BLOCKS)]
    dq, own, *terms, gains = attention(prepared, grad_out[0], window, fan)
    back = {d: shifted(terms[d - 1], -d) for d in (2, 3, 1, 4)}
    gains = exchanged(gains, FAR)
    gains = exchanged(jnp.broadcast_to(gains[None], (near,) + gains.shape), ("y",))
    loss_scale = (lax.axis_size("zl") * lax.axis_size("c") * ctx_count * rows) ** (-0.5)
    dk, dv = finish(own, [back[d] for d in range(1, BLOCKS)], kv, prepared)
    return (dq[None], dk[None], dv[None], gains * loss_scale)


def solution(mesh):
    fine = Mesh(mesh.devices.reshape(2, 2, 8, 4, 4), ("zl", "c", "y", "zh", "x"))
    split = P(("zl", "c"), ("y", "zh"), "x")
    return jax.shard_map(
        on_device,
        mesh=fine,
        in_specs=(split, split, split, split, P(), P(), P(("zl", "c"), None)),
        out_specs=(split, split, split, P()),
        check_vma=False,
    )
```
